512 devices in a mesh: pw: 128 (over x, z_lo, y), band: 4 (over z_hi, core).
Axes of the slice: x: 4, y: 8, z: 8 (z_hi: 2, z_lo: 4; z = z_hi * 4 + z_lo), core: 2. Of those that a mesh axis runs over, the one named last changes fastest.
Arguments:
- orbitals: bfloat16 [163840, 512], P('pw', 'band'), may hold values from -0.296875 to 0.296875
- exchange_vectors: bfloat16 [163840, 2048], P('pw', 'band'), may hold values from -0.296875 to 0.296875
- cotangent: bfloat16 [163840, 512], P('pw', 'band'), may hold values from -0.1875 to 0.1875
Outputs:
- orbital_grad: bfloat16 [163840, 512], P('pw', 'band')
- vector_grad: bfloat16 [163840, 2048], P('pw', 'band')
The draws below stay inside these ranges and needn't reach their ends.
All inputs are finite; a program needn't handle non-finite values.
Results may differ from the reference program's by a relative error of at most 0.013.
Values may be sent and summed in bfloat16 or wider, within the bound.
A program may use at most 64 MiB of HBM per device.

```python
import jax
import jax.numpy as jnp
from jax import lax

PW_DEV = 1280
NXI = 2048
NPSI = 512
NPW = 163840
N_PW = 128
N_BAND = 4


def block_scale(stream_key, dims, pieces, least, largest):
    gain = 1.0
    for position, parts in pieces:
        steps = jax.random.uniform(jax.random.fold_in(jax.random.fold_in(stream_key, 6), position), (parts,), jnp.float32, least / len(pieces), largest / len(pieces))
        gain = gain * jnp.repeat(jnp.exp(steps), dims[position] // parts).reshape((-1,) + (1,) * (len(dims) - 1 - position))
    return gain


def centred(rng, dims, spread, reach, shards=(), held_as=jnp.bfloat16):
    factor_of = block_scale(rng, dims, shards, -0.22, 0.18) if shards else 1.0
    result = jax.random.normal(rng, dims, jnp.float32) * spread * factor_of
    return jnp.minimum(jnp.maximum(result, -reach), reach).astype(held_as)


def setup_inputs(seed: int = 0) -> dict:
    splits = jax.random.split(jax.random.key(seed), 4)
    orbitals = centred(splits[0], (NPW, NPSI), (NPW ** -0.25), 0.296875, ((0, 128), (1, 4)))
    exchange_vectors = centred(splits[1], (NPW, NXI), (NPW ** -0.25), 0.296875, ((0, 128), (1, 4)))
    cotangent = centred(splits[2], (NPW, NPSI), (2 * NPSI) ** -0.5, 0.1875, ((0, 128), (1, 4)))
    return {"orbitals": orbitals, "exchange_vectors": exchange_vectors, "cotangent": cotangent}


def contract_rows(left, right):
    return lax.dot_general(left, right, (((0,), (0,)), ((), ())), preferred_element_type=jnp.float32)


def contract_cols(left, right):
    return lax.dot_general(left, right, (((1,), (1,)), ((), ())), preferred_element_type=jnp.float32)


def reference(orbitals, exchange_vectors, cotangent):
    projections = contract_rows(exchange_vectors, orbitals).astype(jnp.bfloat16)
    cotangent_proj = contract_rows(exchange_vectors, cotangent).astype(jnp.bfloat16)
    block_width = NXI // N_BAND

    def per_rows(blocks):
        orbital_rows, vector_rows, cotangent_rows = blocks
        vector_part = (contract_cols(cotangent_rows, projections) + contract_cols(orbital_rows, cotangent_proj)).astype(jnp.bfloat16)
        running = jnp.zeros((orbital_rows.shape[0], NPSI), jnp.float32)
        for block_index in range(N_BAND):
            lower = block_index * block_width
            term = jnp.dot(vector_rows[:, lower:lower + block_width], cotangent_proj[lower:lower + block_width], preferred_element_type=jnp.float32).astype(jnp.bfloat16)
            term = lax.optimization_barrier(term)
            running = running + term.astype(jnp.float32)
        return running.astype(jnp.bfloat16), vector_part

    orbital_blocks, vector_blocks = lax.map(per_rows, (orbitals.reshape(N_PW, PW_DEV, NPSI), exchange_vectors.reshape(N_PW, PW_DEV, NXI), cotangent.reshape(N_PW, PW_DEV, NPSI)))
    return orbital_blocks.reshape(N_PW * PW_DEV, NPSI), vector_blocks.reshape(N_PW * PW_DEV, NXI)
```

```python
import jax
import jax.numpy as jnp
from jax import lax
from jax.experimental import pallas as pl
from jax.experimental.pallas import tpu as pltpu
from jax.sharding import PartitionSpec as P

MESH = pl.DeviceIdType.MESH
BF, F32 = jnp.bfloat16, jnp.float32
NX, NY, NZ = 4, 8, 4
ROWS, HALF, NXI_DEV, LANES = 1280, 640, 512, 128
DMA = pltpu.SemaphoreType.DMA
CHUNKS = {"e": 512, "c0": 128, "c1": 128, "p0": 128, "p1": 128}
AR_BUFFERS = ("part", "rx", "sx", "ry", "sy", "rz", "full")
N_STAGES = 5


def dot_nn(left, right):
    return lax.dot_general(left, right, (((1,), (0,)), ((), ())), preferred_element_type=F32)


def dot_nt(left, right):
    return lax.dot_general(left, right, (((1,), (1,)), ((), ())), preferred_element_type=F32)


def send(src, dst, send_sem, recv_sem, device):
    copy = pltpu.make_async_remote_copy(
        src_ref=src,
        dst_ref=dst,
        send_sem=send_sem,
        recv_sem=recv_sem,
        device_id=device,
        device_id_type=MESH,
    )
    copy.start()
    return copy


class Chunk:
    def __init__(self, width, refs, here):
        self.width = width
        self.part, self.rx, self.sx, self.ry, self.sy, self.rz, self.full, self.ss, self.rs = refs
        self.here = here

    def _wait(self, stage, like, which):
        copy = pltpu.make_async_remote_copy(
            src_ref=like,
            dst_ref=like,
            send_sem=self.ss.at[stage],
            recv_sem=self.rs.at[stage],
            device_id=self.here.mate,
            device_id_type=MESH,
        )
        if which == "recv":
            copy.wait_recv()
        else:
            copy.wait_send()

    def start(self, partial):
        h = self.here
        self.part[...] = partial.astype(BF).reshape(NX, NY, 16, self.width)
        for d in (2, 1, 3):
            send(self.part.at[(h.x + d) % NX], self.rx.at[d - 1], self.ss.at[0], self.rs.at[0], h.at(dx=d))

    def after_x(self):
        h = self.here
        self._wait(0, self.rx, "recv")
        total = self.part[h.x].astype(F32)
        for d in range(NX - 1):
            total += self.rx[d].astype(F32)
        self.sx[...] = total.astype(BF)
        for d in (4, 3, 5, 2, 6, 1, 7):
            send(self.sx.at[(h.y + d) % NY], self.ry.at[d - 1], self.ss.at[1], self.rs.at[1], h.at(dy=d))

    def after_y(self):
        h = self.here
        self._wait(1, self.ry, "recv")
        total = self.sx[h.y].astype(F32)
        for d in range(NY - 1):
            total += self.ry[d].astype(F32)
        self.sy[...] = total.astype(BF)
        for d in (2, 1, 3):
            send(self.sy, self.rz.at[d - 1], self.ss.at[2], self.rs.at[2], h.at(dz=d))

    def after_z(self):
        h = self.here
        self._wait(2, self.rz, "recv")
        total = self.sy[...].astype(F32)
        for d in range(NZ - 1):
            total += self.rz[d].astype(F32)
        self.full[h.x, h.y] = total.astype(BF)
        mine = self.full.at[h.x, h.y]
        for d in (4, 3, 5, 2, 6, 1, 7):
            send(mine, mine, self.ss.at[3], self.rs.at[3], h.at(dy=d))

    def after_gather_y(self):
        h = self.here
        self._wait(3, self.ry, "recv")
        mine = self.full.at[h.x]
        for d in (2, 1, 3):
            send(mine, mine, self.ss.at[4], self.rs.at[4], h.at(dx=d))

    def after_gather_x(self):
        self._wait(4, self.rx, "recv")

    def drain(self):
        self._wait(0, self.rx, "send")
        self._wait(1, self.ry, "send")
        self._wait(2, self.rz, "send")
        self._wait(3, self.ry, "send")
        self._wait(4, self.rx, "send")

    def value(self):
        return self.full[...].reshape(NXI_DEV, self.width)

    def columns(self, j):
        return self.full[:, :, :, j * LANES : (j + 1) * LANES].reshape(NXI_DEV, LANES)


class Here:
    def __init__(self):
        pw, band = lax.axis_index("pw"), lax.axis_index("band")
        self.x, self.z, self.y = pw // (NZ * NY), (pw // NY) % NZ, pw % NY
        self.zh, self.core = band // 2, band % 2
        self.pw = pw
        self.mate = (pw, self.zh * 2 + (1 - self.core))
        self.band = band

    def at(self, dx=0, dy=0, dz=0):
        x, y, z = (self.x + dx) % NX, (self.y + dy) % NY, (self.z + dz) % NZ
        return ((x * NZ + z) * NY + y, self.band)

    def across(self, core):
        return (self.pw, (1 - self.zh) * 2 + core)


def kernel(orb_hbm, xv_hbm, cot_hbm, og_hbm, vg_hbm, *scratch):
    names = ["xv", "xt", "cn", "pn", "cz", "pz", "acc", "vg", "te", "tm", "tl", "tlm", "ts", "ogz", "og"]
    names += ["loc", "ms", "mr", "zs", "zr", "ls", "lr", "es", "er", "fs", "fr", "gs", "gr", "out"]
    s = dict(zip(names, scratch))
    rest = scratch[len(names) :]
    here = Here()
    core = here.core
    per = len(AR_BUFFERS) + 2
    ch = {n: Chunk(w, rest[i * per : (i + 1) * per], here) for i, (n, w) in enumerate(CHUNKS.items())}

    barrier = pltpu.get_barrier_semaphore()
    peers = [here.at(dx=d) for d in (1, 2, 3)] + [here.at(dy=d) for d in range(1, 8)]
    peers += [here.at(dz=d) for d in (1, 2, 3)] + [here.mate, here.across(0), here.across(1)]
    for peer in peers:
        pl.semaphore_signal(barrier, inc=1, device_id=peer, device_id_type=MESH)

    def local(src, dst, sem):
        copy = pltpu.make_async_copy(src, dst, sem)
        copy.start()
        return copy

    loads = []
    for half in range(2):
        rows = pl.ds(half * HALF, HALF)
        loads.append(local(xv_hbm.at[rows], s["xv"].at[rows], s["loc"].at[half]))
    for half in range(2):
        rows = pl.ds(half * HALF, HALF)
        loads.append(local(cot_hbm.at[rows], s["cn"].at[core, half], s["loc"].at[2 + half]))
        loads.append(local(orb_hbm.at[rows], s["pn"].at[core, half], s["loc"].at[4 + half]))
    for load in loads:
        load.wait()
    s["xt"][...] = s["xv"][...].T

    pl.semaphore_wait(barrier, len(peers))

    to_mate = [
        send(s["cn"].at[core], s["cn"].at[core], s["ms"].at[0], s["mr"].at[0], here.mate),
        send(s["pn"].at[core], s["pn"].at[core], s["ms"].at[1], s["mr"].at[1], here.mate),
    ]

    across = here.across(core)

    def send_z(k):
        src, dst = (s["cn"], s["cz"]) if k < 2 else (s["pn"], s["pz"])
        return send(src.at[k % 2, core], dst.at[k % 2, core], s["zs"].at[k], s["zr"].at[k], across)

    def relay(k):
        z_sent[k].wait_recv()
        dst = s["cz"] if k < 2 else s["pz"]
        return send(dst.at[k % 2, core], dst.at[k % 2, core], s["ls"].at[k], s["lr"].at[k], here.mate)

    def panel(name, j):
        return s[name][j].reshape(ROWS, LANES)

    to_mate[0].wait_recv()
    z_sent = [send_z(0), send_z(1)]
    to_mate[1].wait_recv()
    near = jnp.concatenate([panel("cn", 0), panel("cn", 1), panel("pn", 0), panel("pn", 1)], axis=1)
    ch["e"].start(dot_nn(s["xt"][...], near))

    ch["e"].after_x()
    z_sent[0].wait_send()
    z_sent.append(send_z(2))
    relays = [relay(0)]
    relays[0].wait_recv()
    ch["c0"].start(dot_nn(s["xt"][...], panel("cz", 0)))
    ch["e"].after_y()
    z_sent[1].wait_send()
    z_sent.append(send_z(3))
    relays.append(relay(1))
    ch["c0"].after_x()
    relays[1].wait_recv()
    ch["c1"].start(dot_nn(s["xt"][...], panel("cz", 1)))
    ch["e"].after_z()
    ch["c0"].after_y()
    relays.append(relay(2))
    ch["c1"].after_x()
    relays[2].wait_recv()
    ch["p0"].start(dot_nn(s["xt"][...], panel("pz", 0)))
    ch["c0"].after_z()
    ch["e"].after_gather_y()
    ch["c1"].after_y()
    relays.append(relay(3))
    ch["c0"].after_gather_y()
    relays[3].wait_recv()
    ch["p1"].start(dot_nn(s["xt"][...], panel("pz", 1)))
    ch["p0"].after_x()
    ch["c1"].after_z()

    terms_m, terms_z = [], []

    def term(j):
        ch[f"c{j}"].after_gather_x()
        value = dot_nn(s["xv"][...], ch[f"c{j}"].value())
        s["tl"][j] = value.astype(BF).reshape(2, HALF, LANES)
        terms_m.append(send(s["tl"].at[j, 1 - core], s["tlm"].at[j], s["fs"].at[j], s["fr"].at[j], here.mate))

    def term_out(j):
        terms_m[j].wait_recv()
        total = s["tl"][j, core].astype(F32) + s["tlm"][j].astype(F32)
        s["ts"][j] = total.astype(BF)
        terms_z.append(send(s["ts"].at[j], s["ogz"].at[core], s["gs"].at[j], s["gr"].at[0], here.across(j)))

    term(0)
    ch["c1"].after_gather_y()
    term_out(0)
    ch["p0"].after_y()
    ch["p1"].after_x()
    ch["e"].after_gather_x()

    for j in range(2):
        s["te"][j] = dot_nn(s["xv"][...], ch["e"].columns(j)).astype(BF)
    to_mate.append(send(s["te"].at[1 - core], s["tm"], s["es"].at[0], s["er"].at[0], here.mate))
    term(1)
    ch["p0"].after_z()
    term_out(1)

    tile = 256

    def rows_of(name, j, i):
        parts = []
        for k in range(tile // 128):
            at = i * tile + k * 128
            parts.append(s[name][j, at // HALF, at % HALF : at % HALF + 128])
        return jnp.concatenate(parts, axis=0)

    for i in range(ROWS // tile):
        left = jnp.concatenate(
            [rows_of("pn", 0, i), rows_of("pn", 1, i), rows_of("cn", 0, i), rows_of("cn", 1, i)], axis=1
        )
        s["acc"][i * tile : (i + 1) * tile] = dot_nt(left, ch["e"].value())
    ch["p1"].after_y()
    ch["p0"].after_gather_y()
    late = jnp.concatenate([ch["c0"].value(), ch["c1"].value()], axis=1)
    for i in range(ROWS // tile):
        left = jnp.concatenate([rows_of("pz", 0, i), rows_of("pz", 1, i)], axis=1)
        s["acc"][i * tile : (i + 1) * tile] += dot_nt(left, late)
    ch["p1"].after_z()
    to_mate[2].wait_recv()
    ch["p1"].after_gather_y()
    ch["p0"].after_gather_x()
    ch["p1"].after_gather_x()

    late = jnp.concatenate([ch["p0"].value(), ch["p1"].value()], axis=1)
    stores = []
    for i in range(ROWS // tile):
        rows = pl.ds(i * tile, tile)
        left = jnp.concatenate([rows_of("cz", 0, i), rows_of("cz", 1, i)], axis=1)
        s["vg"][rows] = (s["acc"][rows] + dot_nt(left, late)).astype(BF)
        stores.append(local(s["vg"].at[rows], vg_hbm.at[rows], s["out"].at[i]))

    copy = pltpu.make_async_remote_copy(
        src_ref=s["ogz"],
        dst_ref=s["ogz"],
        send_sem=s["gs"].at[0],
        recv_sem=s["gr"].at[0],
        device_id=here.mate,
        device_id_type=MESH,
    )
    copy.wait_recv()
    total = s["te"][core].astype(F32) + s["tm"][...].astype(F32) + s["ogz"][...].reshape(ROWS, LANES).astype(F32)
    s["og"][...] = total.astype(BF)
    stores.append(local(s["og"], og_hbm, s["out"].at[ROWS // tile]))

    for copy in to_mate + z_sent[2:] + relays + terms_m + terms_z:
        copy.wait_send()
    for c in ch.values():
        c.drain()
    for store in stores:
        store.wait()


def body(orbitals, exchange_vectors, cotangent):
    panel = pltpu.VMEM((2, 2, HALF, LANES), BF)
    scratch = [
        pltpu.VMEM((ROWS, NXI_DEV), BF),
        pltpu.VMEM((NXI_DEV, ROWS), BF),
        panel,
        panel,
        panel,
        panel,
        pltpu.VMEM((ROWS, NXI_DEV), F32),
        pltpu.VMEM((ROWS, NXI_DEV), BF),
        pltpu.VMEM((2, ROWS, LANES), BF),
        pltpu.VMEM((ROWS, LANES), BF),
        panel,
        pltpu.VMEM((2, HALF, LANES), BF),
        pltpu.VMEM((2, HALF, LANES), BF),
        pltpu.VMEM((2, HALF, LANES), BF),
        pltpu.VMEM((ROWS, LANES), BF),
        DMA((6,)),
        DMA((2,)),
        DMA((2,)),
        DMA((4,)),
        DMA((4,)),
        DMA((4,)),
        DMA((4,)),
        DMA((1,)),
        DMA((1,)),
        DMA((2,)),
        DMA((2,)),
        DMA((2,)),
        DMA((1,)),
        DMA((6,)),
    ]
    for width in CHUNKS.values():
        scratch += [
            pltpu.VMEM((NX, NY, 16, width), BF),
            pltpu.VMEM((NX - 1, NY, 16, width), BF),
            pltpu.VMEM((NY, 16, width), BF),
            pltpu.VMEM((NY - 1, 16, width), BF),
            pltpu.VMEM((16, width), BF),
            pltpu.VMEM((NZ - 1, 16, width), BF),
            pltpu.VMEM((NX, NY, 16, width), BF),
            DMA((N_STAGES,)),
            DMA((N_STAGES,)),
        ]
    anywhere = pl.BlockSpec(memory_space=pl.ANY)
    return pl.pallas_call(
        kernel,
        out_shape=(
            jax.ShapeDtypeStruct((ROWS, LANES), BF),
            jax.ShapeDtypeStruct((ROWS, NXI_DEV), BF),
        ),
        in_specs=[anywhere] * 3,
        out_specs=(anywhere, anywhere),
        scratch_shapes=scratch,
        name="exchange_backward",
        compiler_params=pltpu.CompilerParams(
            collective_id=0, has_side_effects=True, vmem_limit_bytes=48 << 20
        ),
        cost_estimate=pl.CostEstimate(flops=3400000000, bytes_accessed=4000000, transcendentals=0),
    )(orbitals, exchange_vectors, cotangent)


def solution(mesh):
    placed = (P("pw", "band"), P("pw", "band"), P("pw", "band"))
    return jax.shard_map(
        body,
        mesh=mesh,
        in_specs=placed,
        out_specs=(P("pw", "band"), P("pw", "band")),
        check_vma=False,
    )
```

```python
import jax
import jax.numpy as jnp
from jax import lax
from jax.experimental import pallas as pl
from jax.experimental.pallas import tpu as pltpu
from jax.sharding import PartitionSpec as P

MESH = pl.DeviceIdType.MESH
BF, F32 = jnp.bfloat16, jnp.float32
NX, NY, NZ = 4, 8, 4
ROWS, HALF, NXI_DEV, LANES = 1280, 640, 512, 128
DMA = pltpu.SemaphoreType.DMA
CHUNKS = {"e": 512, "c0": 128, "c1": 128, "p": 256}
AR_BUFFERS = ("part", "rx", "sx", "ry", "sy", "rz", "full")
N_STAGES = 5


def dot_tn(left, right):
    return lax.dot_general(left, right, (((0,), (0,)), ((), ())), preferred_element_type=F32)


def dot_nn(left, right):
    return lax.dot_general(left, right, (((1,), (0,)), ((), ())), preferred_element_type=F32)


def dot_nt(left, right):
    return lax.dot_general(left, right, (((1,), (1,)), ((), ())), preferred_element_type=F32)


def send(src, dst, send_sem, recv_sem, device):
    copy = pltpu.make_async_remote_copy(
        src_ref=src,
        dst_ref=dst,
        send_sem=send_sem,
        recv_sem=recv_sem,
        device_id=device,
        device_id_type=MESH,
    )
    copy.start()
    return copy


class Chunk:
    def __init__(self, width, refs, here):
        self.width = width
        self.part, self.rx, self.sx, self.ry, self.sy, self.rz, self.full, self.ss, self.rs = refs
        self.here = here

    def _wait(self, stage, like, which):
        copy = pltpu.make_async_remote_copy(
            src_ref=like,
            dst_ref=like,
            send_sem=self.ss.at[stage],
            recv_sem=self.rs.at[stage],
            device_id=self.here.mate,
            device_id_type=MESH,
        )
        if which == "recv":
            copy.wait_recv()
        else:
            copy.wait_send()

    def start(self, partial):
        h = self.here
        self.part[...] = partial.astype(BF).reshape(NX, NY, 16, self.width)
        for d in (2, 1, 3):
            send(self.part.at[(h.x + d) % NX], self.rx.at[d - 1], self.ss.at[0], self.rs.at[0], h.at(dx=d))

    def after_x(self):
        h = self.here
        self._wait(0, self.rx, "recv")
        total = self.part[h.x].astype(F32)
        for d in range(NX - 1):
            total += self.rx[d].astype(F32)
        self.sx[...] = total.astype(BF)
        for d in (4, 3, 5, 2, 6, 1, 7):
            send(self.sx.at[(h.y + d) % NY], self.ry.at[d - 1], self.ss.at[1], self.rs.at[1], h.at(dy=d))

    def after_y(self):
        h = self.here
        self._wait(1, self.ry, "recv")
        total = self.sx[h.y].astype(F32)
        for d in range(NY - 1):
            total += self.ry[d].astype(F32)
        self.sy[...] = total.astype(BF)
        for d in (2, 1, 3):
            send(self.sy, self.rz.at[d - 1], self.ss.at[2], self.rs.at[2], h.at(dz=d))

    def after_z(self):
        h = self.here
        self._wait(2, self.rz, "recv")
        total = self.sy[...].astype(F32)
        for d in range(NZ - 1):
            total += self.rz[d].astype(F32)
        self.full[h.x, h.y] = total.astype(BF)
        mine = self.full.at[h.x, h.y]
        for d in (4, 3, 5, 2, 6, 1, 7):
            send(mine, mine, self.ss.at[3], self.rs.at[3], h.at(dy=d))

    def after_gather_y(self):
        h = self.here
        self._wait(3, self.ry, "recv")
        mine = self.full.at[h.x]
        for d in (2, 1, 3):
            send(mine, mine, self.ss.at[4], self.rs.at[4], h.at(dx=d))

    def after_gather_x(self):
        self._wait(4, self.rx, "recv")

    def drain(self):
        self._wait(0, self.rx, "send")
        self._wait(1, self.ry, "send")
        self._wait(2, self.rz, "send")
        self._wait(3, self.ry, "send")
        self._wait(4, self.rx, "send")

    def value(self):
        return self.full[...].reshape(NXI_DEV, self.width)

    def columns(self, j):
        return self.full[:, :, :, j * LANES : (j + 1) * LANES].reshape(NXI_DEV, LANES)


class Here:
    def __init__(self):
        pw, band = lax.axis_index("pw"), lax.axis_index("band")
        self.x, self.z, self.y = pw // (NZ * NY), (pw // NY) % NZ, pw % NY
        self.zh, self.core = band // 2, band % 2
        self.mate = (pw, self.zh * 2 + (1 - self.core))
        self.pw = pw
        self.band = band

    def at(self, dx=0, dy=0, dz=0):
        x, y, z = (self.x + dx) % NX, (self.y + dy) % NY, (self.z + dz) % NZ
        return ((x * NZ + z) * NY + y, self.band)

    def across(self, core):
        return (self.pw, (1 - self.zh) * 2 + core)


SCRATCH = ("xv", "cn", "pn", "cz", "pz", "acc", "te", "tm", "tz", "tzm", "ts", "ogz")
SEMS = {"load": 3, "ms": 3, "mr": 3, "zs": 3, "zr": 3, "ls": 3, "lr": 3}
SEMS.update({"es": 1, "er": 1, "fs": 2, "fr": 2, "gs": 2, "gr": 1})
PIECES = (8, 2)


def kernel(orb_hbm, xv_hbm, cot_hbm, og, vg, *scratch):
    names = SCRATCH + tuple(SEMS)
    s = dict(zip(names, scratch))
    rest = scratch[len(names) :]
    here = Here()
    per = len(AR_BUFFERS) + 2
    ch = {n: Chunk(w, rest[i * per : (i + 1) * per], here) for i, (n, w) in enumerate(CHUNKS.items())}
    e, p, late = ch["e"], ch["p"], (ch["c0"], ch["c1"])
    core = here.core
    xv, cn, pn, cz, pz = s["xv"], s["cn"], s["pn"], s["cz"], s["pz"]

    barrier = pltpu.get_barrier_semaphore()
    peers = [here.across(0), here.across(1)] + [here.at(dy=d) for d in range(1, 8)] + [here.at(dx=d) for d in (1, 2, 3)]
    peers += [here.at(dz=d) for d in (1, 2, 3)] + [here.mate]
    for peer in peers:
        pl.semaphore_signal(barrier, inc=1, device_id=peer, device_id_type=MESH)

    loads = [
        pltpu.make_async_copy(cot_hbm, cn.at[0], s["load"].at[0]),
        pltpu.make_async_copy(orb_hbm, pn.at[0], s["load"].at[1]),
        pltpu.make_async_copy(xv_hbm, xv, s["load"].at[2]),
    ]
    for load in loads:
        load.start()
    loads[0].wait()
    loads[1].wait()
    pl.semaphore_wait(barrier, len(peers))

    def remote(src, dst, kind, k, device):
        return send(src, dst, s[kind + "s"].at[k], s[kind + "r"].at[k], device)

    def waiter(like, kind, k):
        return pltpu.make_async_remote_copy(
            src_ref=like,
            dst_ref=like,
            send_sem=s[kind + "s"].at[k],
            recv_sem=s[kind + "r"].at[k],
            device_id=here.mate,
            device_id_type=MESH,
        )

    opposite = here.across(core)
    mine, others = pl.ds(core * HALF, HALF), pl.ds((1 - core) * HALF, HALF)
    m_cot = [
        remote(cn.at[0, others], cn.at[1, others], "m", 0, here.mate),
        remote(cn.at[0, mine], cn.at[1, mine], "m", 1, here.mate),
    ]
    m_orb = remote(pn.at[0], pn.at[1], "m", 2, here.mate)
    m_cot[0].wait_recv()
    for j in range(2):
        size = HALF // PIECES[j]
        for i in range(PIECES[j]):
            rows = pl.ds(core * HALF + i * size, size)
            remote(cn.at[(core + j) % 2, rows], cz.at[j, rows], "z", j, opposite)
    z_cot = [waiter(cz.at[j, mine], "z", j) for j in range(2)]
    loads[2].wait()
    m_cot[1].wait_recv()
    m_orb.wait_recv()
    e.start(dot_tn(xv[...], jnp.concatenate([cn[0], cn[1], pn[0], pn[1]], axis=1)))
    e.after_x()
    z_cot[0].wait_send()
    z_orb = remote(pn.at[0], pz.at[core], "z", 2, opposite)

    def relay(j):
        z_cot[j].wait_recv()
        return remote(cz.at[j, mine], cz.at[j, mine], "l", j, here.mate)

    def start_late(j):
        l_cot[j].wait_recv()
        late[j].start(dot_tn(xv[...], cz[j]))

    terms_m, terms_z = [], []

    def term(j):
        s["tz"][j] = dot_nn(xv[...], late[j].value()).astype(BF)
        terms_m.append(remote(s["tz"].at[j, others], s["tzm"].at[j], "f", j, here.mate))

    def term_out(j):
        terms_m[j].wait_recv()
        s["ts"][j] = (s["tz"][j, mine].astype(F32) + s["tzm"][j].astype(F32)).astype(BF)
        terms_z.append(send(s["ts"].at[j], s["ogz"].at[mine], s["gs"].at[j], s["gr"].at[0], here.across(j)))

    l_cot = [relay(0)]
    start_late(0)
    e.after_y()
    late[0].after_x()
    l_cot.append(relay(1))
    start_late(1)
    late[0].after_y()
    late[1].after_x()
    late[0].after_z()
    late[1].after_y()
    z_orb.wait_recv()
    l_orb = remote(pz.at[core], pz.at[core], "l", 2, here.mate)
    late[0].after_gather_y()
    l_orb.wait_recv()
    p.start(dot_tn(xv[...], jnp.concatenate([pz[0], pz[1]], axis=1)))
    late[1].after_z()
    late[0].after_gather_x()
    term(0)
    p.after_x()
    e.after_z()
    term_out(0)
    late[1].after_gather_y()
    e.after_gather_y()
    p.after_y()
    late[1].after_gather_x()
    term(1)
    term_out(1)

    tile = 256
    tiles = [pl.ds(i * tile, tile) for i in range(ROWS // tile)]
    cproj = jnp.concatenate([late[0].value(), late[1].value()], axis=1)
    for rows in tiles:
        left = jnp.concatenate([pz[0, rows], pz[1, rows]], axis=1)
        s["acc"][rows] = dot_nt(left, cproj)
    p.after_z()
    e.after_gather_x()

    for j in range(2):
        s["te"][1 - j] = dot_nn(xv[...], e.columns(1 - j)).astype(BF)
        if j == 0:
            m_term = remote(s["te"].at[1], s["tm"], "e", 0, here.mate)
    p.after_gather_y()
    for rows in tiles:
        left = jnp.concatenate([pn[0, rows], pn[1, rows], cn[0, rows], cn[1, rows]], axis=1)
        s["acc"][rows] += dot_nt(left, e.value())
    m_term.wait_recv()
    p.after_gather_x()
    for rows in tiles:
        left = jnp.concatenate([cz[0, rows], cz[1, rows]], axis=1)
        vg[rows] = (s["acc"][rows] + dot_nt(left, p.value())).astype(BF)

    waiter(s["ogz"], "g", 0).wait_recv()
    total = s["te"][0].astype(F32) + s["tm"][...].astype(F32) + s["ogz"][...].astype(F32)
    og[...] = total.astype(BF)

    for copy in m_cot + [m_orb, z_cot[1], z_orb, l_orb, m_term] + l_cot + terms_m + terms_z:
        copy.wait_send()
    for chunk in ch.values():
        chunk.drain()


def body(orbitals, exchange_vectors, cotangent):
    panels = pltpu.VMEM((2, ROWS, LANES), BF)
    one = pltpu.VMEM((ROWS, LANES), BF)
    halves = pltpu.VMEM((2, HALF, LANES), BF)
    shapes = {
        "xv": pltpu.VMEM((ROWS, NXI_DEV), BF),
        "cn": panels,
        "pn": panels,
        "cz": panels,
        "pz": panels,
        "acc": pltpu.VMEM((ROWS, NXI_DEV), F32),
        "te": panels,
        "tm": one,
        "tz": panels,
        "tzm": halves,
        "ts": halves,
        "ogz": one,
    }
    scratch = [shapes[name] for name in SCRATCH] + [DMA((n,)) for n in SEMS.values()]
    for width in CHUNKS.values():
        scratch += [
            pltpu.VMEM((NX, NY, 16, width), BF),
            pltpu.VMEM((NX - 1, NY, 16, width), BF),
            pltpu.VMEM((NY, 16, width), BF),
            pltpu.VMEM((NY - 1, 16, width), BF),
            pltpu.VMEM((16, width), BF),
            pltpu.VMEM((NZ - 1, 16, width), BF),
            pltpu.VMEM((NX, NY, 16, width), BF),
            DMA((N_STAGES,)),
            DMA((N_STAGES,)),
        ]
    return pl.pallas_call(
        kernel,
        out_shape=(
            jax.ShapeDtypeStruct((ROWS, LANES), BF),
            jax.ShapeDtypeStruct((ROWS, NXI_DEV), BF),
        ),
        in_specs=[pl.BlockSpec(memory_space=pltpu.HBM)] * 3,
        out_specs=(pl.BlockSpec(memory_space=pltpu.VMEM), pl.BlockSpec(memory_space=pltpu.VMEM)),
        scratch_shapes=scratch,
        name="exchange_backward",
        compiler_params=pltpu.CompilerParams(
            collective_id=0, has_side_effects=True, vmem_limit_bytes=205 << 18
        ),
        cost_estimate=pl.CostEstimate(flops=3400000000, bytes_accessed=4000000, transcendentals=0),
    )(orbitals, exchange_vectors, cotangent)


def solution(mesh):
    placed = (P("pw", "band"), P("pw", "band"), P("pw", "band"))
    return jax.shard_map(
        body,
        mesh=mesh,
        in_specs=placed,
        out_specs=(P("pw", "band"), P("pw", "band")),
        check_vma=False,
    )
```

```python
import jax
import jax.numpy as jnp
from jax import lax
from jax.experimental import pallas as pl
from jax.experimental.pallas import tpu as pltpu
from jax.sharding import PartitionSpec as P

MESH = pl.DeviceIdType.MESH
BF, F32 = jnp.bfloat16, jnp.float32
NX, NY, NZ = 4, 8, 4
ROWS, HALF, NXI_DEV, LANES = 1280, 640, 512, 128
DMA = pltpu.SemaphoreType.DMA
CHUNKS = {"e": 512, "c0": 128, "c1": 128, "p": 256}
AR_BUFFERS = ("part", "rx", "sx", "ry", "sy", "rz", "full")
N_STAGES = 5
TILE = 256


def dot_tn(left, right):
    return lax.dot_general(left, right, (((0,), (0,)), ((), ())), preferred_element_type=F32)


def dot_nn(left, right):
    return lax.dot_general(left, right, (((1,), (0,)), ((), ())), preferred_element_type=F32)


def dot_nt(left, right):
    return lax.dot_general(left, right, (((1,), (1,)), ((), ())), preferred_element_type=F32)


def send(src, dst, send_sem, recv_sem, device):
    copy = pltpu.make_async_remote_copy(
        src_ref=src,
        dst_ref=dst,
        send_sem=send_sem,
        recv_sem=recv_sem,
        device_id=device,
        device_id_type=MESH,
    )
    copy.start()
    return copy


class Chunk:
    def __init__(self, width, refs, here):
        self.width = width
        self.part, self.rx, self.sx, self.ry, self.sy, self.rz, self.full, self.ss, self.rs = refs
        self.here = here

    def _wait(self, stage, like, which):
        copy = pltpu.make_async_remote_copy(
            src_ref=like,
            dst_ref=like,
            send_sem=self.ss.at[stage],
            recv_sem=self.rs.at[stage],
            device_id=self.here.mate,
            device_id_type=MESH,
        )
        if which == "recv":
            copy.wait_recv()
        else:
            copy.wait_send()

    def start(self, partial):
        h = self.here
        self.part[...] = partial.astype(BF).reshape(NX, NY, 16, self.width)
        for d in (2, 1, 3):
            send(self.part.at[(h.x + d) % NX], self.rx.at[d - 1], self.ss.at[0], self.rs.at[0], h.at(dx=d))

    def after_x(self):
        h = self.here
        self._wait(0, self.rx, "recv")
        total = self.part[h.x].astype(F32)
        for d in range(NX - 1):
            total += self.rx[d].astype(F32)
        self.sx[...] = total.astype(BF)
        for d in (4, 3, 5, 2, 6, 1, 7):
            send(self.sx.at[(h.y + d) % NY], self.ry.at[d - 1], self.ss.at[1], self.rs.at[1], h.at(dy=d))

    def after_y(self):
        h = self.here
        self._wait(1, self.ry, "recv")
        total = self.sx[h.y].astype(F32)
        for d in range(NY - 1):
            total += self.ry[d].astype(F32)
        self.sy[...] = total.astype(BF)
        for d in (2, 1, 3):
            send(self.sy, self.rz.at[d - 1], self.ss.at[2], self.rs.at[2], h.at(dz=d))

    def after_z(self):
        h = self.here
        self._wait(2, self.rz, "recv")
        total = self.sy[...].astype(F32)
        for d in range(NZ - 1):
            total += self.rz[d].astype(F32)
        self.full[h.x, h.y] = total.astype(BF)
        mine = self.full.at[h.x, h.y]
        for d in (4, 3, 5, 2, 6, 1, 7):
            send(mine, mine, self.ss.at[3], self.rs.at[3], h.at(dy=d))

    def after_gather_y(self):
        h = self.here
        self._wait(3, self.ry, "recv")
        mine = self.full.at[h.x]
        for d in (2, 1, 3):
            send(mine, mine, self.ss.at[4], self.rs.at[4], h.at(dx=d))

    def after_gather_x(self):
        self._wait(4, self.rx, "recv")

    def drain(self):
        self._wait(0, self.rx, "send")
        self._wait(1, self.ry, "send")
        self._wait(2, self.rz, "send")
        self._wait(3, self.ry, "send")
        self._wait(4, self.rx, "send")

    def value(self):
        return self.full[...].reshape(NXI_DEV, self.width)

    def columns(self, j):
        return self.full[:, :, :, j * LANES : (j + 1) * LANES].reshape(NXI_DEV, LANES)


class Here:
    def __init__(self):
        pw, band = lax.axis_index("pw"), lax.axis_index("band")
        self.x, self.z, self.y = pw // (NZ * NY), (pw // NY) % NZ, pw % NY
        self.zh, self.core = band // 2, band % 2
        self.mate = (pw, self.zh * 2 + (1 - self.core))
        self.pw = pw
        self.band = band

    def at(self, dx=0, dy=0, dz=0):
        x, y, z = (self.x + dx) % NX, (self.y + dy) % NY, (self.z + dz) % NZ
        return ((x * NZ + z) * NY + y, self.band)

    def across(self, core):
        return (self.pw, (1 - self.zh) * 2 + core)


SCRATCH = ("xv", "cn", "pn", "cz", "pz", "acc", "te", "tm", "tz", "tzm", "ts", "ogz")
SEMS = {"load": 3, "ms": 3, "mr": 3, "zs": 3, "zr": 3, "ls": 3, "lr": 3}
SEMS.update({"es": 1, "er": 1, "fs": 2, "fr": 2, "gs": 2, "gr": 1})
PIECES = (8, 2)


def kernel(orb_hbm, xv_hbm, cot_hbm, og, vg, *scratch):
    names = SCRATCH + tuple(SEMS)
    s = dict(zip(names, scratch))
    rest = scratch[len(names) :]
    here = Here()
    per = len(AR_BUFFERS) + 2
    ch = {n: Chunk(w, rest[i * per : (i + 1) * per], here) for i, (n, w) in enumerate(CHUNKS.items())}
    e, p, late = ch["e"], ch["p"], (ch["c0"], ch["c1"])
    core = here.core
    xv, cn, pn, cz, pz = s["xv"], s["cn"], s["pn"], s["cz"], s["pz"]

    barrier = pltpu.get_barrier_semaphore()
    peers = [here.across(0), here.across(1)] + [here.at(dy=d) for d in range(1, 8)] + [here.at(dx=d) for d in (1, 2, 3)]
    peers += [here.at(dz=d) for d in (1, 2, 3)] + [here.mate]
    for peer in peers:
        pl.semaphore_signal(barrier, inc=1, device_id=peer, device_id_type=MESH)

    loads = [
        pltpu.make_async_copy(cot_hbm, cn.at[0], s["load"].at[0]),
        pltpu.make_async_copy(orb_hbm, pn.at[0], s["load"].at[1]),
        pltpu.make_async_copy(xv_hbm, xv, s["load"].at[2]),
    ]
    for load in loads:
        load.start()
    loads[0].wait()
    loads[1].wait()
    pl.semaphore_wait(barrier, len(peers))

    def remote(src, dst, kind, k, device):
        return send(src, dst, s[kind + "s"].at[k], s[kind + "r"].at[k], device)

    def waiter(like, kind, k):
        return pltpu.make_async_remote_copy(
            src_ref=like,
            dst_ref=like,
            send_sem=s[kind + "s"].at[k],
            recv_sem=s[kind + "r"].at[k],
            device_id=here.mate,
            device_id_type=MESH,
        )

    opposite = here.across(core)
    mine, others = pl.ds(core * HALF, HALF), pl.ds((1 - core) * HALF, HALF)
    m_cot = [
        remote(cn.at[0, others], cn.at[1, others], "m", 0, here.mate),
        remote(cn.at[0, mine], cn.at[1, mine], "m", 1, here.mate),
    ]
    m_orb = remote(pn.at[0], pn.at[1], "m", 2, here.mate)
    m_cot[0].wait_recv()
    for j in range(2):
        size = HALF // PIECES[j]
        for i in range(PIECES[j]):
            rows = pl.ds(core * HALF + i * size, size)
            remote(cn.at[(core + j) % 2, rows], cz.at[j, rows], "z", j, opposite)
    z_cot = [waiter(cz.at[j, mine], "z", j) for j in range(2)]
    loads[2].wait()
    m_cot[1].wait_recv()
    m_orb.wait_recv()
    def relay(j):
        z_cot[j].wait_recv()
        return remote(cz.at[j, mine], cz.at[j, mine], "l", j, here.mate)

    def start_late(j):
        l_cot[j].wait_recv()
        late[j].start(dot_tn(xv[...], cz[j]))

    terms_m, terms_z = [], []

    def term(j):
        s["tz"][j] = dot_nn(xv[...], late[j].value()).astype(BF)
        terms_m.append(remote(s["tz"].at[j, others], s["tzm"].at[j], "f", j, here.mate))

    def term_out(j):
        terms_m[j].wait_recv()
        s["ts"][j] = (s["tz"][j, mine].astype(F32) + s["tzm"][j].astype(F32)).astype(BF)
        terms_z.append(send(s["ts"].at[j], s["ogz"].at[mine], s["gs"].at[j], s["gr"].at[0], here.across(j)))


    tiles = [pl.ds(i * TILE, TILE) for i in range(ROWS // TILE)]
    added = []

    def add_to_grad(panels, right, last=False):
        for rows in tiles:
            total = dot_nt(jnp.concatenate([ref[k, rows] for ref, k in panels], axis=1), right)
            if added:
                total += s["acc"][rows]
            if last:
                vg[rows] = total.astype(BF)
            else:
                s["acc"][rows] = total
        added.append(right)

    e.start(dot_tn(xv[...], jnp.concatenate([cn[0], cn[1], pn[0], pn[1]], axis=1)))
    e.after_x()
    z_cot[0].wait_send()
    z_orb = remote(pn.at[0], pz.at[core], "z", 2, opposite)
    l_cot = [relay(0)]
    l_cot.append(relay(1))
    start_late(0)
    start_late(1)
    late[0].after_x()
    late[1].after_x()
    late[0].after_y()
    e.after_y()
    z_orb.wait_recv()
    l_orb = remote(pz.at[core], pz.at[core], "l", 2, here.mate)
    late[1].after_y()
    late[0].after_z()
    l_orb.wait_recv()
    p.start(dot_tn(xv[...], jnp.concatenate([pz[0], pz[1]], axis=1)))
    late[1].after_z()
    late[0].after_gather_y()
    p.after_x()
    e.after_z()
    late[0].after_gather_x()
    term(0)
    late[1].after_gather_y()
    p.after_y()
    term_out(0)
    p.after_z()
    e.after_gather_y()
    late[1].after_gather_x()
    add_to_grad([(pz, 0), (pz, 1)], jnp.concatenate([late[0].value(), late[1].value()], axis=1))
    term(1)
    term_out(1)
    p.after_gather_y()
    e.after_gather_x()
    add_to_grad([(pn, 0), (pn, 1), (cn, 0), (cn, 1)], e.value())
    for k in (1, 0):
        s["te"][k] = dot_nn(xv[...], e.columns(k)).astype(BF)
        if k == 1:
            m_term = remote(s["te"].at[1], s["tm"], "e", 0, here.mate)
    p.after_gather_x()
    add_to_grad([(cz, 0), (cz, 1)], p.value(), last=True)
    m_term.wait_recv()
    waiter(s["ogz"], "g", 0).wait_recv()
    total = s["te"][0].astype(F32) + s["tm"][...].astype(F32) + s["ogz"][...].astype(F32)
    og[...] = total.astype(BF)

    for copy in m_cot + [m_orb, z_cot[1], z_orb, l_orb, m_term] + l_cot + terms_m + terms_z:
        copy.wait_send()
    for chunk in ch.values():
        chunk.drain()


def body(orbitals, exchange_vectors, cotangent):
    panels = pltpu.VMEM((2, ROWS, LANES), BF)
    one = pltpu.VMEM((ROWS, LANES), BF)
    halves = pltpu.VMEM((2, HALF, LANES), BF)
    shapes = {
        "xv": pltpu.VMEM((ROWS, NXI_DEV), BF),
        "cn": panels,
        "pn": panels,
        "cz": panels,
        "pz": panels,
        "acc": pltpu.VMEM((ROWS, NXI_DEV), F32),
        "te": panels,
        "tm": one,
        "tz": panels,
        "tzm": halves,
        "ts": halves,
        "ogz": one,
    }
    scratch = [shapes[name] for name in SCRATCH] + [DMA((n,)) for n in SEMS.values()]
    for width in CHUNKS.values():
        scratch += [
            pltpu.VMEM((NX, NY, 16, width), BF),
            pltpu.VMEM((NX - 1, NY, 16, width), BF),
            pltpu.VMEM((NY, 16, width), BF),
            pltpu.VMEM((NY - 1, 16, width), BF),
            pltpu.VMEM((16, width), BF),
            pltpu.VMEM((NZ - 1, 16, width), BF),
            pltpu.VMEM((NX, NY, 16, width), BF),
            DMA((N_STAGES,)),
            DMA((N_STAGES,)),
        ]
    return pl.pallas_call(
        kernel,
        out_shape=(
            jax.ShapeDtypeStruct((ROWS, LANES), BF),
            jax.ShapeDtypeStruct((ROWS, NXI_DEV), BF),
        ),
        in_specs=[pl.BlockSpec(memory_space=pltpu.HBM)] * 3,
        out_specs=(pl.BlockSpec(memory_space=pltpu.VMEM), pl.BlockSpec(memory_space=pltpu.VMEM)),
        scratch_shapes=scratch,
        name="exchange_backward",
        compiler_params=pltpu.CompilerParams(
            collective_id=0, has_side_effects=True, vmem_limit_bytes=205 << 18
        ),
        cost_estimate=pl.CostEstimate(flops=3400000000, bytes_accessed=4000000, transcendentals=0),
    )(orbitals, exchange_vectors, cotangent)


def solution(mesh):
    placed = (P("pw", "band"), P("pw", "band"), P("pw", "band"))
    return jax.shard_map(
        body,
        mesh=mesh,
        in_specs=placed,
        out_specs=(P("pw", "band"), P("pw", "band")),
        check_vma=False,
    )
```

```python
import jax
import jax.numpy as jnp
from jax import lax
from jax.experimental import pallas as pl
from jax.experimental.pallas import tpu as pltpu
from jax.sharding import PartitionSpec as P

MESH = pl.DeviceIdType.MESH
BF, F32 = jnp.bfloat16, jnp.float32
NX, NY, NZ = 4, 8, 4
ROWS, HALF, NXI_DEV, LANES = 1280, 640, 512, 128
DMA = pltpu.SemaphoreType.DMA
CHUNKS = {"e": 512, "c0": 128, "c1": 128, "p0": 128, "p1": 128}
AR_BUFFERS = ("part", "rx", "sx", "ry", "sy", "rz", "full")
N_STAGES = 5
TILE = 256


def dot_tn(left, right):
    return lax.dot_general(left, right, (((0,), (0,)), ((), ())), preferred_element_type=F32)


def dot_nn(left, right):
    return lax.dot_general(left, right, (((1,), (0,)), ((), ())), preferred_element_type=F32)


def dot_nt(left, right):
    return lax.dot_general(left, right, (((1,), (1,)), ((), ())), preferred_element_type=F32)


def send(src, dst, send_sem, recv_sem, device):
    copy = pltpu.make_async_remote_copy(
        src_ref=src,
        dst_ref=dst,
        send_sem=send_sem,
        recv_sem=recv_sem,
        device_id=device,
        device_id_type=MESH,
    )
    copy.start()
    return copy


class Chunk:
    def __init__(self, width, refs, here):
        self.width = width
        self.part, self.rx, self.sx, self.ry, self.sy, self.rz, self.full, self.ss, self.rs = refs
        self.here = here

    def _wait(self, stage, like, which):
        copy = pltpu.make_async_remote_copy(
            src_ref=like,
            dst_ref=like,
            send_sem=self.ss.at[stage],
            recv_sem=self.rs.at[stage],
            device_id=self.here.mate,
            device_id_type=MESH,
        )
        if which == "recv":
            copy.wait_recv()
        else:
            copy.wait_send()

    def start(self, partial):
        h = self.here
        self.part[...] = partial.astype(BF).reshape(NX, NY, 16, self.width)
        for d in (2, 1, 3):
            send(self.part.at[(h.x + d) % NX], self.rx.at[d - 1], self.ss.at[0], self.rs.at[0], h.at(dx=d))

    def after_x(self):
        h = self.here
        self._wait(0, self.rx, "recv")
        total = self.part[h.x].astype(F32)
        for d in range(NX - 1):
            total += self.rx[d].astype(F32)
        self.sx[...] = total.astype(BF)
        for d in (4, 3, 5, 2, 6, 1, 7):
            send(self.sx.at[(h.y + d) % NY], self.ry.at[d - 1], self.ss.at[1], self.rs.at[1], h.at(dy=d))

    def after_y(self):
        h = self.here
        self._wait(1, self.ry, "recv")
        total = self.sx[h.y].astype(F32)
        for d in range(NY - 1):
            total += self.ry[d].astype(F32)
        self.sy[...] = total.astype(BF)
        for d in (2, 1, 3):
            send(self.sy, self.rz.at[d - 1], self.ss.at[2], self.rs.at[2], h.at(dz=d))

    def after_z(self):
        h = self.here
        self._wait(2, self.rz, "recv")
        total = self.sy[...].astype(F32)
        for d in range(NZ - 1):
            total += self.rz[d].astype(F32)
        self.full[h.x, h.y] = total.astype(BF)
        mine = self.full.at[h.x, h.y]
        for d in (4, 3, 5, 2, 6, 1, 7):
            send(mine, mine, self.ss.at[3], self.rs.at[3], h.at(dy=d))

    def after_gather_y(self):
        h = self.here
        self._wait(3, self.ry, "recv")
        mine = self.full.at[h.x]
        for d in (2, 1, 3):
            send(mine, mine, self.ss.at[4], self.rs.at[4], h.at(dx=d))

    def after_gather_x(self):
        self._wait(4, self.rx, "recv")

    def drain(self):
        self._wait(0, self.rx, "send")
        self._wait(1, self.ry, "send")
        self._wait(2, self.rz, "send")
        self._wait(3, self.ry, "send")
        self._wait(4, self.rx, "send")

    def value(self):
        return self.full[...].reshape(NXI_DEV, self.width)

    def columns(self, j):
        return self.full[:, :, :, j * LANES : (j + 1) * LANES].reshape(NXI_DEV, LANES)


class Here:
    def __init__(self):
        pw, band = lax.axis_index("pw"), lax.axis_index("band")
        self.x, self.z, self.y = pw // (NZ * NY), (pw // NY) % NZ, pw % NY
        self.zh, self.core = band // 2, band % 2
        self.mate = (pw, self.zh * 2 + (1 - self.core))
        self.pw = pw
        self.band = band

    def at(self, dx=0, dy=0, dz=0):
        x, y, z = (self.x + dx) % NX, (self.y + dy) % NY, (self.z + dz) % NZ
        return ((x * NZ + z) * NY + y, self.band)

    def across(self, core):
        return (self.pw, (1 - self.zh) * 2 + core)


SCRATCH = ("xv", "cn", "pn", "cz", "pz", "acc", "te", "tm", "tz", "tzm", "ts", "ogz")
SEMS = {"load": 3, "ms": 3, "mr": 3, "zs": 4, "zr": 4, "ls": 4, "lr": 4}
SEMS.update({"es": 1, "er": 1, "fs": 2, "fr": 2, "gs": 2, "gr": 1})
PIECES = (8, 2)


def kernel(orb_hbm, xv_hbm, cot_hbm, og, vg, *scratch):
    names = SCRATCH + tuple(SEMS)
    s = dict(zip(names, scratch))
    rest = scratch[len(names) :]
    here = Here()
    per = len(AR_BUFFERS) + 2
    ch = {n: Chunk(w, rest[i * per : (i + 1) * per], here) for i, (n, w) in enumerate(CHUNKS.items())}
    e, late, last = ch["e"], (ch["c0"], ch["c1"]), (ch["p0"], ch["p1"])
    core = here.core
    xv, cn, pn, cz, pz = s["xv"], s["cn"], s["pn"], s["cz"], s["pz"]

    barrier = pltpu.get_barrier_semaphore()
    peers = [here.across(0), here.across(1)] + [here.at(dy=d) for d in range(1, 8)] + [here.at(dx=d) for d in (1, 2, 3)]
    peers += [here.at(dz=d) for d in (1, 2, 3)] + [here.mate]
    for peer in peers:
        pl.semaphore_signal(barrier, inc=1, device_id=peer, device_id_type=MESH)

    loads = [
        pltpu.make_async_copy(cot_hbm, cn.at[0], s["load"].at[0]),
        pltpu.make_async_copy(orb_hbm, pn.at[0], s["load"].at[1]),
        pltpu.make_async_copy(xv_hbm, xv, s["load"].at[2]),
    ]
    for load in loads:
        load.start()
    loads[0].wait()
    loads[1].wait()
    pl.semaphore_wait(barrier, len(peers))

    def remote(src, dst, kind, k, device):
        return send(src, dst, s[kind + "s"].at[k], s[kind + "r"].at[k], device)

    def waiter(like, kind, k):
        return pltpu.make_async_remote_copy(
            src_ref=like,
            dst_ref=like,
            send_sem=s[kind + "s"].at[k],
            recv_sem=s[kind + "r"].at[k],
            device_id=here.mate,
            device_id_type=MESH,
        )

    opposite = here.across(core)
    mine, others = pl.ds(core * HALF, HALF), pl.ds((1 - core) * HALF, HALF)
    m_cot = [
        remote(cn.at[0, others], cn.at[1, others], "m", 0, here.mate),
        remote(cn.at[0, mine], cn.at[1, mine], "m", 1, here.mate),
    ]
    m_orb = remote(pn.at[0], pn.at[1], "m", 2, here.mate)
    m_cot[0].wait_recv()
    for j in range(2):
        size = HALF // PIECES[j]
        for i in range(PIECES[j]):
            rows = pl.ds(core * HALF + i * size, size)
            remote(cn.at[(core + j) % 2, rows], cz.at[j, rows], "z", j, opposite)
    z_cot = [waiter(cz.at[j, mine], "z", j) for j in range(2)]
    loads[2].wait()
    m_cot[1].wait_recv()
    m_orb.wait_recv()
    def relay(j):
        z_cot[j].wait_recv()
        return remote(cz.at[j, mine], cz.at[j, mine], "l", j, here.mate)

    def start_late(j):
        l_cot[j].wait_recv()
        late[j].start(dot_tn(xv[...], cz[j]))

    terms_m, terms_z = [], []

    def term(j):
        s["tz"][j] = dot_nn(xv[...], late[j].value()).astype(BF)
        terms_m.append(remote(s["tz"].at[j, others], s["tzm"].at[j], "f", j, here.mate))

    def term_out(j):
        terms_m[j].wait_recv()
        s["ts"][j] = (s["tz"][j, mine].astype(F32) + s["tzm"][j].astype(F32)).astype(BF)
        terms_z.append(send(s["ts"].at[j], s["ogz"].at[mine], s["gs"].at[j], s["gr"].at[0], here.across(j)))


    z_orb = []

    def send_orb(j):
        z_cot[j].wait_send()
        z_orb.append(remote(pn.at[(core + j) % 2, mine], pz.at[j, mine], "z", 2 + j, opposite))

    def relay_orb(j):
        z_orb[j].wait_recv()
        return remote(pz.at[j, mine], pz.at[j, mine], "l", 2 + j, here.mate)

    def start_last(j):
        l_orb[j].wait_recv()
        last[j].start(dot_tn(xv[...], pz[j]))

    tiles = [pl.ds(i * TILE, TILE) for i in range(ROWS // TILE)]
    added = []

    def add_to_grad(panels, right, final=False):
        for rows in tiles:
            total = dot_nt(jnp.concatenate([ref[k, rows] for ref, k in panels], axis=1), right)
            if added:
                total += s["acc"][rows]
            if final:
                vg[rows] = total.astype(BF)
            else:
                s["acc"][rows] = total
        added.append(right)

    e.start(dot_tn(xv[...], jnp.concatenate([cn[0], cn[1], pn[0], pn[1]], axis=1)))
    send_orb(0)
    l_cot = [relay(0)]
    e.after_x()
    start_late(0)
    send_orb(1)
    late[0].after_x()
    l_cot.append(relay(1))
    start_late(1)
    l_orb = [relay_orb(0)]
    start_last(0)
    e.after_y()
    late[0].after_y()
    late[1].after_x()
    late[0].after_z()
    l_orb.append(relay_orb(1))
    last[0].after_x()
    start_last(1)
    late[1].after_y()
    e.after_z()
    late[0].after_gather_y()
    last[0].after_y()
    late[1].after_z()
    last[1].after_x()
    late[0].after_gather_x()
    last[0].after_z()
    term(0)
    late[1].after_gather_y()
    last[1].after_y()
    term_out(0)
    e.after_gather_y()
    late[1].after_gather_x()
    term(1)
    term_out(1)
    last[1].after_z()
    add_to_grad([(pz, 0), (pz, 1)], jnp.concatenate([late[0].value(), late[1].value()], axis=1))
    e.after_gather_x()
    last[0].after_gather_y()
    add_to_grad([(pn, 0), (pn, 1), (cn, 0), (cn, 1)], e.value())
    last[1].after_gather_y()
    for k in (1, 0):
        s["te"][k] = dot_nn(xv[...], e.columns(k)).astype(BF)
        if k == 1:
            m_term = remote(s["te"].at[1], s["tm"], "e", 0, here.mate)
    last[0].after_gather_x()
    last[1].after_gather_x()
    add_to_grad([(cz, 0), (cz, 1)], jnp.concatenate([last[0].value(), last[1].value()], axis=1), final=True)
    m_term.wait_recv()
    waiter(s["ogz"], "g", 0).wait_recv()
    total = s["te"][0].astype(F32) + s["tm"][...].astype(F32) + s["ogz"][...].astype(F32)
    og[...] = total.astype(BF)

    for copy in m_cot + [m_orb, m_term] + z_orb + l_orb + l_cot + terms_m + terms_z:
        copy.wait_send()
    for chunk in ch.values():
        chunk.drain()


def body(orbitals, exchange_vectors, cotangent):
    panels = pltpu.VMEM((2, ROWS, LANES), BF)
    one = pltpu.VMEM((ROWS, LANES), BF)
    halves = pltpu.VMEM((2, HALF, LANES), BF)
    shapes = {
        "xv": pltpu.VMEM((ROWS, NXI_DEV), BF),
        "cn": panels,
        "pn": panels,
        "cz": panels,
        "pz": panels,
        "acc": pltpu.VMEM((ROWS, NXI_DEV), F32),
        "te": panels,
        "tm": one,
        "tz": panels,
        "tzm": halves,
        "ts": halves,
        "ogz": one,
    }
    scratch = [shapes[name] for name in SCRATCH] + [DMA((n,)) for n in SEMS.values()]
    for width in CHUNKS.values():
        scratch += [
            pltpu.VMEM((NX, NY, 16, width), BF),
            pltpu.VMEM((NX - 1, NY, 16, width), BF),
            pltpu.VMEM((NY, 16, width), BF),
            pltpu.VMEM((NY - 1, 16, width), BF),
            pltpu.VMEM((16, width), BF),
            pltpu.VMEM((NZ - 1, 16, width), BF),
            pltpu.VMEM((NX, NY, 16, width), BF),
            DMA((N_STAGES,)),
            DMA((N_STAGES,)),
        ]
    return pl.pallas_call(
        kernel,
        out_shape=(
            jax.ShapeDtypeStruct((ROWS, LANES), BF),
            jax.ShapeDtypeStruct((ROWS, NXI_DEV), BF),
        ),
        in_specs=[pl.BlockSpec(memory_space=pltpu.HBM)] * 3,
        out_specs=(pl.BlockSpec(memory_space=pltpu.VMEM), pl.BlockSpec(memory_space=pltpu.VMEM)),
        scratch_shapes=scratch,
        name="exchange_backward",
        compiler_params=pltpu.CompilerParams(
            collective_id=0, has_side_effects=True, vmem_limit_bytes=205 << 18
        ),
        cost_estimate=pl.CostEstimate(flops=3400000000, bytes_accessed=4000000, transcendentals=0),
    )(orbitals, exchange_vectors, cotangent)


def solution(mesh):
    placed = (P("pw", "band"), P("pw", "band"), P("pw", "band"))
    return jax.shard_map(
        body,
        mesh=mesh,
        in_specs=placed,
        out_specs=(P("pw", "band"), P("pw", "band")),
        check_vma=False,
    )
```

```python
import jax
import jax.numpy as jnp
from jax import lax
from jax.experimental import pallas as pl
from jax.experimental.pallas import tpu as pltpu
from jax.sharding import PartitionSpec as P

MESH = pl.DeviceIdType.MESH
BF, F32 = jnp.bfloat16, jnp.float32
NX, NY, NZ = 4, 8, 4
ROWS, HALF, NXI_DEV, LANES = 1280, 640, 512, 128
DMA = pltpu.SemaphoreType.DMA
CHUNKS = {"e": 512, "c0": 128, "c1": 128, "p0": 128, "p1": 128}
AR_BUFFERS = ("part", "rx", "sx", "ry", "sy", "rz", "full")
N_STAGES = 5
TILE = 256


def dot_tn(left, right):
    return lax.dot_general(left, right, (((0,), (0,)), ((), ())), preferred_element_type=F32)


def dot_nn(left, right):
    return lax.dot_general(left, right, (((1,), (0,)), ((), ())), preferred_element_type=F32)


def dot_nt(left, right):
    return lax.dot_general(left, right, (((1,), (1,)), ((), ())), preferred_element_type=F32)


def send(src, dst, send_sem, recv_sem, device):
    copy = pltpu.make_async_remote_copy(
        src_ref=src,
        dst_ref=dst,
        send_sem=send_sem,
        recv_sem=recv_sem,
        device_id=device,
        device_id_type=MESH,
    )
    copy.start()
    return copy


class Chunk:
    def __init__(self, width, refs, here):
        self.width = width
        self.part, self.rx, self.sx, self.ry, self.sy, self.rz, self.full, self.ss, self.rs = refs
        self.here = here

    def _wait(self, stage, like, which):
        copy = pltpu.make_async_remote_copy(
            src_ref=like,
            dst_ref=like,
            send_sem=self.ss.at[stage],
            recv_sem=self.rs.at[stage],
            device_id=self.here.mate,
            device_id_type=MESH,
        )
        if which == "recv":
            copy.wait_recv()
        else:
            copy.wait_send()

    def start(self, partial):
        h = self.here
        self.part[...] = partial.astype(BF).reshape(NX, NY, 16, self.width)
        for d in (2, 1, 3):
            send(self.part.at[(h.x + d) % NX], self.rx.at[d - 1], self.ss.at[0], self.rs.at[0], h.at(dx=d))

    def after_x(self):
        h = self.here
        self._wait(0, self.rx, "recv")
        total = self.part[h.x].astype(F32)
        for d in range(NX - 1):
            total += self.rx[d].astype(F32)
        self.sx[...] = total.astype(BF)
        for d in (4, 3, 5, 2, 6, 1, 7):
            send(self.sx.at[(h.y + d) % NY], self.ry.at[d - 1], self.ss.at[1], self.rs.at[1], h.at(dy=d))

    def after_y(self):
        h = self.here
        self._wait(1, self.ry, "recv")
        total = self.sx[h.y].astype(F32)
        for d in range(NY - 1):
            total += self.ry[d].astype(F32)
        self.sy[...] = total.astype(BF)
        for d in (2, 1, 3):
            send(self.sy, self.rz.at[d - 1], self.ss.at[2], self.rs.at[2], h.at(dz=d))

    def after_z(self):
        h = self.here
        self._wait(2, self.rz, "recv")
        total = self.sy[...].astype(F32)
        for d in range(NZ - 1):
            total += self.rz[d].astype(F32)
        self.full[h.x, h.y] = total.astype(BF)
        mine = self.full.at[h.x, h.y]
        for d in (4, 3, 5, 2, 6, 1, 7):
            send(mine, mine, self.ss.at[3], self.rs.at[3], h.at(dy=d))

    def after_gather_y(self):
        h = self.here
        self._wait(3, self.ry, "recv")
        mine = self.full.at[h.x]
        for d in (2, 1, 3):
            send(mine, mine, self.ss.at[4], self.rs.at[4], h.at(dx=d))

    def after_gather_x(self):
        self._wait(4, self.rx, "recv")

    def drain(self):
        self._wait(0, self.rx, "send")
        self._wait(1, self.ry, "send")
        self._wait(2, self.rz, "send")
        self._wait(3, self.ry, "send")
        self._wait(4, self.rx, "send")

    def value(self):
        return self.full[...].reshape(NXI_DEV, self.width)

    def columns(self, j):
        return self.full[:, :, :, j * LANES : (j + 1) * LANES].reshape(NXI_DEV, LANES)


class Here:
    def __init__(self):
        pw, band = lax.axis_index("pw"), lax.axis_index("band")
        self.x, self.z, self.y = pw // (NZ * NY), (pw // NY) % NZ, pw % NY
        self.zh, self.core = band // 2, band % 2
        self.mate = (pw, self.zh * 2 + (1 - self.core))
        self.pw = pw
        self.band = band

    def at(self, dx=0, dy=0, dz=0):
        x, y, z = (self.x + dx) % NX, (self.y + dy) % NY, (self.z + dz) % NZ
        return ((x * NZ + z) * NY + y, self.band)

    def across(self, core):
        return (self.pw, (1 - self.zh) * 2 + core)


SCRATCH = ("xv", "cn", "pn", "cz", "pz", "acc", "te", "tm", "tz", "tzm", "ts", "ogz")
SEMS = {"load": 3, "ms": 3, "mr": 3, "zs": 4, "zr": 4, "ls": 4, "lr": 4}
SEMS.update({"es": 1, "er": 1, "fs": 2, "fr": 2, "gs": 2, "gr": 1})
PIECES = (8, 2)


def kernel(orb_hbm, xv_hbm, cot_hbm, og, vg, *scratch):
    names = SCRATCH + tuple(SEMS)
    s = dict(zip(names, scratch))
    rest = scratch[len(names) :]
    here = Here()
    per = len(AR_BUFFERS) + 2
    ch = {n: Chunk(w, rest[i * per : (i + 1) * per], here) for i, (n, w) in enumerate(CHUNKS.items())}
    e, late, last = ch["e"], (ch["c0"], ch["c1"]), (ch["p0"], ch["p1"])
    core = here.core
    xv, cn, pn, cz, pz = s["xv"], s["cn"], s["pn"], s["cz"], s["pz"]

    barrier = pltpu.get_barrier_semaphore()
    peers = [here.across(0), here.across(1)] + [here.at(dy=d) for d in range(1, 8)] + [here.at(dx=d) for d in (1, 2, 3)]
    peers += [here.at(dz=d) for d in (1, 2, 3)] + [here.mate]
    for peer in peers:
        pl.semaphore_signal(barrier, inc=1, device_id=peer, device_id_type=MESH)

    loads = [
        pltpu.make_async_copy(cot_hbm, cn.at[0], s["load"].at[0]),
        pltpu.make_async_copy(orb_hbm, pn.at[0], s["load"].at[1]),
        pltpu.make_async_copy(xv_hbm, xv, s["load"].at[2]),
    ]
    for load in loads:
        load.start()
    loads[0].wait()
    loads[1].wait()
    pl.semaphore_wait(barrier, len(peers))

    def remote(src, dst, kind, k, device):
        return send(src, dst, s[kind + "s"].at[k], s[kind + "r"].at[k], device)

    def waiter(like, kind, k):
        return pltpu.make_async_remote_copy(
            src_ref=like,
            dst_ref=like,
            send_sem=s[kind + "s"].at[k],
            recv_sem=s[kind + "r"].at[k],
            device_id=here.mate,
            device_id_type=MESH,
        )

    opposite = here.across(core)
    mine, others = pl.ds(core * HALF, HALF), pl.ds((1 - core) * HALF, HALF)
    m_cot = [
        remote(cn.at[0, others], cn.at[1, others], "m", 0, here.mate),
        remote(cn.at[0, mine], cn.at[1, mine], "m", 1, here.mate),
    ]
    m_orb = remote(pn.at[0], pn.at[1], "m", 2, here.mate)
    m_cot[0].wait_recv()
    for j in range(2):
        size = HALF // PIECES[j]
        for i in range(PIECES[j]):
            rows = pl.ds(core * HALF + i * size, size)
            remote(cn.at[(core + j) % 2, rows], cz.at[j, rows], "z", j, opposite)
    z_cot = [waiter(cz.at[j, mine], "z", j) for j in range(2)]
    loads[2].wait()
    m_cot[1].wait_recv()
    m_orb.wait_recv()
    def relay(j):
        z_cot[j].wait_recv()
        return remote(cz.at[j, mine], cz.at[j, mine], "l", j, here.mate)

    def start_late(j):
        l_cot[j].wait_recv()
        late[j].start(dot_tn(xv[...], cz[j]))

    terms_m, terms_z = [], []

    def term(j):
        s["tz"][j] = dot_nn(xv[...], late[j].value()).astype(BF)
        terms_m.append(remote(s["tz"].at[j, others], s["tzm"].at[j], "f", j, here.mate))

    def term_out(j):
        terms_m[j].wait_recv()
        s["ts"][j] = (s["tz"][j, mine].astype(F32) + s["tzm"][j].astype(F32)).astype(BF)
        terms_z.append(send(s["ts"].at[j], s["ogz"].at[mine], s["gs"].at[j], s["gr"].at[0], here.across(j)))


    z_orb = []

    def send_orb(j):
        z_cot[j].wait_send()
        z_orb.append(remote(pn.at[(core + j) % 2, mine], pz.at[j, mine], "z", 2 + j, opposite))

    def relay_orb(j):
        z_orb[j].wait_recv()
        return remote(pz.at[j, mine], pz.at[j, mine], "l", 2 + j, here.mate)

    def start_last(j):
        l_orb[j].wait_recv()
        last[j].start(dot_tn(xv[...], pz[j]))

    tiles = [pl.ds(i * TILE, TILE) for i in range(ROWS // TILE)]
    added = []

    def add_to_grad(panels, right, final=False):
        for rows in tiles:
            total = dot_nt(jnp.concatenate([ref[k, rows] for ref, k in panels], axis=1), right)
            if added:
                total += s["acc"][rows]
            if final:
                vg[rows] = total.astype(BF)
            else:
                s["acc"][rows] = total
        added.append(right)

    e.start(dot_tn(xv[...], jnp.concatenate([cn[0], cn[1], pn[0], pn[1]], axis=1)))
    send_orb(0)
    l_cot = [relay(0)]
    e.after_x()
    start_late(0)
    e.after_y()
    send_orb(1)
    late[0].after_x()
    l_cot.append(relay(1))
    start_late(1)
    l_orb = [relay_orb(0)]
    start_last(0)
    late[0].after_y()
    late[1].after_x()
    late[0].after_z()
    l_orb.append(relay_orb(1))
    last[0].after_x()
    start_last(1)
    late[1].after_y()
    e.after_z()
    late[0].after_gather_y()
    last[0].after_y()
    late[1].after_z()
    last[1].after_x()
    late[0].after_gather_x()
    last[0].after_z()
    term(0)
    late[1].after_gather_y()
    last[1].after_y()
    term_out(0)
    e.after_gather_y()
    late[1].after_gather_x()
    term(1)
    term_out(1)
    last[1].after_z()
    add_to_grad([(pz, 0), (pz, 1)], jnp.concatenate([late[0].value(), late[1].value()], axis=1))
    e.after_gather_x()
    last[0].after_gather_y()
    add_to_grad([(pn, 0), (pn, 1), (cn, 0), (cn, 1)], e.value())
    last[1].after_gather_y()
    for k in (1, 0):
        s["te"][k] = dot_nn(xv[...], e.columns(k)).astype(BF)
        if k == 1:
            m_term = remote(s["te"].at[1], s["tm"], "e", 0, here.mate)
    last[0].after_gather_x()
    last[1].after_gather_x()
    add_to_grad([(cz, 0), (cz, 1)], jnp.concatenate([last[0].value(), last[1].value()], axis=1), final=True)
    m_term.wait_recv()
    waiter(s["ogz"], "g", 0).wait_recv()
    total = s["te"][0].astype(F32) + s["tm"][...].astype(F32) + s["ogz"][...].astype(F32)
    og[...] = total.astype(BF)

    for copy in m_cot + [m_orb, m_term] + z_orb + l_orb + l_cot + terms_m + terms_z:
        copy.wait_send()
    for chunk in ch.values():
        chunk.drain()


def body(orbitals, exchange_vectors, cotangent):
    panels = pltpu.VMEM((2, ROWS, LANES), BF)
    one = pltpu.VMEM((ROWS, LANES), BF)
    halves = pltpu.VMEM((2, HALF, LANES), BF)
    shapes = {
        "xv": pltpu.VMEM((ROWS, NXI_DEV), BF),
        "cn": panels,
        "pn": panels,
        "cz": panels,
        "pz": panels,
        "acc": pltpu.VMEM((ROWS, NXI_DEV), F32),
        "te": panels,
        "tm": one,
        "tz": panels,
        "tzm": halves,
        "ts": halves,
        "ogz": one,
    }
    scratch = [shapes[name] for name in SCRATCH] + [DMA((n,)) for n in SEMS.values()]
    for width in CHUNKS.values():
        scratch += [
            pltpu.VMEM((NX, NY, 16, width), BF),
            pltpu.VMEM((NX - 1, NY, 16, width), BF),
            pltpu.VMEM((NY, 16, width), BF),
            pltpu.VMEM((NY - 1, 16, width), BF),
            pltpu.VMEM((16, width), BF),
            pltpu.VMEM((NZ - 1, 16, width), BF),
            pltpu.VMEM((NX, NY, 16, width), BF),
            DMA((N_STAGES,)),
            DMA((N_STAGES,)),
        ]
    return pl.pallas_call(
        kernel,
        out_shape=(
            jax.ShapeDtypeStruct((ROWS, LANES), BF),
            jax.ShapeDtypeStruct((ROWS, NXI_DEV), BF),
        ),
        in_specs=[pl.BlockSpec(memory_space=pltpu.HBM)] * 3,
        out_specs=(pl.BlockSpec(memory_space=pltpu.VMEM), pl.BlockSpec(memory_space=pltpu.VMEM)),
        scratch_shapes=scratch,
        name="exchange_backward",
        compiler_params=pltpu.CompilerParams(
            collective_id=0, has_side_effects=True, vmem_limit_bytes=205 << 18
        ),
        cost_estimate=pl.CostEstimate(flops=3400000000, bytes_accessed=4000000, transcendentals=0),
    )(orbitals, exchange_vectors, cotangent)


def solution(mesh):
    placed = (P("pw", "band"), P("pw", "band"), P("pw", "band"))
    return jax.shard_map(
        body,
        mesh=mesh,
        in_specs=placed,
        out_specs=(P("pw", "band"), P("pw", "band")),
        check_vma=False,
    )
```
